512 devices in a mesh: section: 4 (over y_hi), chan: 16 (over z, core), dp: 8 (over y_lo, x).
Axes of the slice: x: 4, y: 8 (y_hi: 4, y_lo: 2; y = y_hi * 2 + y_lo), z: 8, core: 2. Of those that a mesh axis runs over, the one named last changes fastest.
Arguments:
- images: bfloat16 [2560, 2048], P(('section', 'dp')), may hold values from -6 to 6
- conv_one: bfloat16 [3, 3, 2560, 5120], P(None, None, ('section', 'dp'), 'chan'), may hold values from -0.0390625 to 0.0390625
- conv_two: bfloat16 [3, 3, 5120, 5120], P(None, None, ('section', 'dp'), 'chan'), may hold values from -0.02734375 to 0.02734375
- mix_weight: bfloat16 [5120, 5120], P(('section', 'dp'), 'chan'), may hold values from -0.078125 to 0.078125
Outputs:
- block_out: bfloat16 [8, 64, 5120], P('dp', 'section', 'chan')
The draws below stay inside these ranges and needn't reach their ends.
All inputs are finite; a program needn't handle non-finite values.
Results may differ from the reference program's by a relative error of at most 0.02.
Values may be sent and summed in bfloat16 or wider, within the bound.
A program may use at most 64 MiB of HBM per device.

```python
import jax
import jax.numpy as jnp

C0 = 2560
C = 5120
HW = 16
IMGS = 8
N_SECTION = 4
N_CHAN = 16
N_DP = 8


def level_of(rng, shape, split, low, high):
    factor_of = 1.0
    for position, parts in split:
        steps = jax.random.uniform(jax.random.fold_in(jax.random.fold_in(rng, 6), position), (parts,), jnp.float32, low / len(split), high / len(split))
        factor_of = factor_of * jnp.repeat(jnp.exp(steps), shape[position] // parts).reshape((-1,) + (1,) * (len(shape) - 1 - position))
    return factor_of


def normal_values(rng, extent, scale, most, split=(), held_as=jnp.bfloat16):
    level = level_of(rng, extent, split, -0.22, 0.18) if split else 1.0
    array = jax.random.normal(rng, extent, jnp.float32) * scale * level
    return jnp.minimum(jnp.maximum(array, -most), most).astype(held_as)


def setup_inputs(seed: int = 0) -> dict:
    key_list = jax.random.split(jax.random.key(seed), 5)
    images = normal_values(key_list[0], (C0, IMGS * HW * HW), 1.0, 6.0, ((0, 32),))
    conv_one = normal_values(key_list[1], (3, 3, C0, C), (9 * C0) ** -0.5, 0.0390625, ((2, 32), (3, 16)))
    conv_two = normal_values(key_list[2], (3, 3, C, C), (9 * C) ** -0.5, 0.02734375, ((2, 32), (3, 16)))
    mix_weight = normal_values(key_list[3], (C, C), C ** -0.5, 0.078125, ((0, 32), (1, 16)))
    return dict(images=images, conv_one=conv_one, conv_two=conv_two, mix_weight=mix_weight)


def reference(images, conv_one, conv_two, mix_weight):
    side = HW
    count = images.shape[1] // (side * side)
    half = side // 2
    rows = count * half * half
    groups_one = N_SECTION * N_DP
    groups_two = N_CHAN
    maps = images.reshape(images.shape[0], count, side, side).transpose(1, 2, 3, 0)
    padded = jnp.pad(maps, ((0, 0), (1, 1), (1, 1), (0, 0)))
    windows = []
    for tap_a in range(3):
        for tap_b in range(3):
            windows.append(padded[:, tap_a:tap_a + side:2, tap_b:tap_b + side:2, :].reshape(rows, -1))
    width_one = conv_one.shape[2] // groups_one
    total = jnp.zeros((rows, conv_one.shape[3]), jnp.float32)
    for group in range(groups_one):
        low = group * width_one
        partial_sum = jnp.zeros((rows, conv_one.shape[3]), jnp.float32)
        for tap_a in range(3):
            for tap_b in range(3):
                window = windows[tap_a * 3 + tap_b][:, low:low + width_one]
                partial_sum = partial_sum + jnp.dot(window, conv_one[tap_a, tap_b, low:low + width_one], preferred_element_type=jnp.float32)
        total = total + partial_sum.astype(jnp.bfloat16).astype(jnp.float32)
    hidden = total.astype(jnp.bfloat16)
    rectified = jnp.maximum(hidden, 0).reshape(count, half, half, -1)
    padded_two = jnp.pad(rectified, ((0, 0), (1, 1), (1, 1), (0, 0)))
    width_two = conv_two.shape[3] // groups_two
    inner = jnp.zeros((rows, conv_two.shape[2]), jnp.float32)
    for group in range(groups_two):
        low = group * width_two
        partial_sum = jnp.zeros((rows, conv_two.shape[2]), jnp.float32)
        for tap_a in range(3):
            for tap_b in range(3):
                window = padded_two[:, tap_a:tap_a + half, tap_b:tap_b + half, low:low + width_two].reshape(rows, -1)
                partial_sum = partial_sum + jnp.dot(window, conv_two[tap_a, tap_b, :, low:low + width_two].T, preferred_element_type=jnp.float32)
        inner = inner + partial_sum.astype(jnp.bfloat16).astype(jnp.float32)
    gated = jnp.maximum(inner, 0.0).astype(jnp.bfloat16)
    width_mix = mix_weight.shape[0] // groups_one
    mixed = hidden.astype(jnp.float32)
    for group in range(groups_one):
        low = group * width_mix
        partial_sum = jnp.dot(gated[:, low:low + width_mix], mix_weight[low:low + width_mix], preferred_element_type=jnp.float32)
        mixed = mixed + partial_sum.astype(jnp.bfloat16).astype(jnp.float32)
    return mixed.astype(jnp.bfloat16).reshape(count, half * half, -1)
```

```python
import functools

import jax
import jax.numpy as jnp
from jax import lax
from jax.experimental import pallas as pl
from jax.experimental.pallas import tpu as pltpu
from jax.sharding import PartitionSpec as P

MESH = pl.DeviceIdType.MESH
BF16 = jnp.bfloat16
F32 = jnp.float32
NX, NY, NC = 4, 8, 16
HALVES = (0, 1)
ORDER = (1, 0)
FAR_FIRST = (8, 7, 9, 6, 10, 5, 11, 4, 12, 3, 13, 2, 14, 1, 15)
FORWARD = (1, 7, 2, 6, 3, 5, 4)


def nt(a, b):
    return lax.dot_general(a, b, (((1,), (1,)), ((), ())), preferred_element_type=F32)


def selection():
    row = lax.broadcasted_iota(jnp.int32, (192, 768), 0)
    col = lax.broadcasted_iota(jnp.int32, (192, 768), 1)
    a, i, j = row >> 6, (row >> 3) & 7, row & 7
    b, place = col >> 8, col & 255
    wanted = (2 * i + a - 1) * 16 + 2 * j + b - 1
    inside = jnp.logical_or(j > 0, b > 0)
    hit = jnp.logical_and(wanted == place, inside)
    return jnp.where(hit, 1.0, 0.0).astype(BF16)


def kernel(
    images, conv_one, conv_two, mix_weight, out,
    maps, w1, w2, wm, sel, lhs, snd1, rcvx1, ybuf1, rcvy1, hid, zsnd, rcvz, gat,
    snd3, rcvx3, ybuf3, rcvy3, load_sem, send_sem, rx1, ry1, ay, ax, rz, az, rx3, ry3,
):
    s, c, d = lax.axis_index("section"), lax.axis_index("chan"), lax.axis_index("dp")
    x = d % NX
    y = s * 2 + d // NX
    par = y % 2
    quarter = y // 2

    def at_x(k):
        return (s, c, (d // NX) * NX + (x + k) % NX)

    def at_y(k):
        to = (y + k) % NY
        return (to // 2, c, (to % 2) * NX + x)

    def at_c(k):
        return (s, (c + k) % NC, d)

    loads = [
        pltpu.make_async_copy(images.at[:, pl.ds(pl.multiple_of(par * 1024, 1024), 1024)], maps.at[0], load_sem.at[0]),
        pltpu.make_async_copy(conv_one, w1, load_sem.at[2]),
        pltpu.make_async_copy(images.at[:, pl.ds(pl.multiple_of((1 - par) * 1024, 1024), 1024)], maps.at[1], load_sem.at[1]),
        pltpu.make_async_copy(conv_two, w2, load_sem.at[3]),
        pltpu.make_async_copy(mix_weight, wm, load_sem.at[4]),
    ]
    for copy in loads:
        copy.start()

    barrier = pltpu.get_barrier_semaphore()
    for k in (4, 3, 5, 2, 6, 1, 7):
        pl.semaphore_signal(barrier, 1, device_id=at_y(k), device_id_type=MESH)
    for k in FAR_FIRST:
        pl.semaphore_signal(barrier, 1, device_id=at_c(k), device_id_type=MESH)
    for k in range(1, NX):
        pl.semaphore_signal(barrier, 1, device_id=at_x(k), device_id_type=MESH)

    def send(src, dst, which, sem, to):
        pltpu.make_async_remote_copy(
            src_ref=src, dst_ref=dst, send_sem=send_sem.at[which], recv_sem=sem, device_id=to, device_id_type=MESH
        ).start()

    def wait(ref, sem):
        pltpu.make_async_copy(ref, ref, sem).wait()

    def distance(g, r):
        return (4 - g + 2 * r) % NY

    def send_x(g, snd, rcvx, rx, which):
        for r in range(4):
            q = ((y + distance(g, r)) % NY) // 2
            for k in (2, 1, 3):
                send(snd.at[g, (x + k) % NX, q], rcvx.at[g, r, k - 1], which, rx.at[g, r], at_x(k))

    def send_y(g, snd, rcvx, rx, ybuf, rcvy, ry, which):
        own = None
        for r in range(4):
            k = distance(g, r)
            q = ((y + k) % NY) // 2
            wait(rcvx.at[g, r], rx.at[g, r])
            total = snd[g, x, q].astype(F32)
            for other in range(NX - 1):
                total = total + rcvx[g, r, other].astype(F32)
            if k == 0:
                own = total
            else:
                ybuf[g, r] = total.astype(BF16)
                send(ybuf.at[g, r], rcvy.at[k - 1], which, ry, at_y(k))
        return own

    sel[...] = selection()
    zero = jnp.zeros((80, 256), BF16)
    for g in HALVES:
        loads[0 if g == 0 else 2].wait()
        for n in range(4):
            one = maps[g, :, n * 256 : (n + 1) * 256]
            spread = jnp.concatenate(
                [
                    jnp.concatenate([one, zero, zero], 1),
                    jnp.concatenate([zero, one, zero], 1),
                    jnp.concatenate([zero, zero, one], 1),
                ],
                0,
            )
            windows = nt(sel[...], spread).astype(BF16)
            for a in range(3):
                lhs[a, n * 64 : (n + 1) * 64] = windows[a * 64 : (a + 1) * 64]
        if g == 0:
            loads[1].wait()
        total = jnp.zeros((256, 320), F32)
        for a in range(3):
            total = total + jnp.dot(lhs[a], w1[a].reshape(240, 320), preferred_element_type=F32)
        snd1[g] = total.astype(BF16).reshape(4, 4, 16, 320)
        if g == 0:
            pl.semaphore_wait(barrier, (NX - 1) + (NY - 1) + (NC - 1))
        send_x(g, snd1, rcvx1, rx1, 0)

    own = None
    for g in HALVES:
        got = send_y(g, snd1, rcvx1, rx1, ybuf1, rcvy1, ry1, 1)
        own = got if own is None else own
    wait(rcvy1, ry1)
    for k in range(NY - 1):
        own = own + rcvy1[k].astype(F32)
    mine = own.astype(BF16)
    hid[0, x, quarter] = mine

    for k in (4, 3, 5, 2, 6, 1, 7):
        here = hid.at[0, x, quarter]
        send(here, hid.at[k % 2, x, quarter], 2, ay.at[k - 1], at_y(k))

    def forward(g, q):
        for k in (2, 1, 3):
            send(hid.at[g, x, q], hid.at[g, x, q], 3, ax.at[g], at_x(k))

    forward(0, quarter)
    for k in FORWARD:
        q = ((y - k + NY) % NY) // 2
        wait(hid.at[k % 2, x, q], ay.at[k - 1])
        forward(k % 2, q)

    loads[3].wait()
    for g in ORDER:
        wait(hid.at[g, 0:3], ax.at[g])
        rect = jnp.maximum(hid[g].reshape(256, 320).astype(F32), 0.0).reshape(32, 8, 320)
        place = lax.broadcasted_iota(jnp.int32, (32, 8, 320), 1)
        left = jnp.where(place == 0, 0.0, pltpu.roll(rect, 1, 1))
        right = jnp.where(place == 7, 0.0, pltpu.roll(rect, 7, 1))
        shifted = [v.reshape(256, 320).astype(BF16) for v in (left, rect, right)]
        parts = []
        for a in range(3):
            acc = jnp.zeros((256, 160), F32)
            for b in range(3):
                acc = acc + nt(shifted[b], w2[a, b])
            parts.append(acc.reshape(4, 64, 160))
        gap = jnp.zeros((4, 8, 160), F32)
        inner = (
            parts[1]
            + jnp.concatenate([gap, parts[0][:, :56]], 1)
            + jnp.concatenate([parts[2][:, 8:], gap], 1)
        )
        zsnd[g] = inner.astype(BF16).reshape(16, 16, 160)
        for k in FAR_FIRST:
            send(zsnd.at[g, (c + k) % NC], rcvz.at[g, k - 1], 4, rz.at[g], at_c(k))

    for g in ORDER:
        wait(rcvz.at[g], rz.at[g])
        total = zsnd[g, c].astype(F32)
        for k in range(NC - 1):
            total = total + rcvz[g, k].astype(F32)
        gat[g, c] = jnp.maximum(total, 0.0).astype(BF16)
        for k in FAR_FIRST:
            send(gat.at[g, c], gat.at[g, c], 4, az.at[g], at_c(k))

    loads[4].wait()
    for g in ORDER:
        wait(gat.at[g, 0 : NC - 1], az.at[g])
        mixed = jnp.dot(gat[g].reshape(256, 160), wm[...], preferred_element_type=F32)
        snd3[g] = mixed.astype(BF16).reshape(4, 4, 16, 320)
        send_x(g, snd3, rcvx3, rx3, 0)
    own = None
    for g in ORDER:
        got = send_y(g, snd3, rcvx3, rx3, ybuf3, rcvy3, ry3, 1)
        own = got if own is None else own
    wait(rcvy3, ry3)
    for k in range(NY - 1):
        own = own + rcvy3[k].astype(F32)
    out[0] = (own + mine.astype(F32)).astype(BF16)

    for _ in range(2):
        wait(snd1.at[:, 0:3], send_sem.at[0])
        wait(rcvy1, send_sem.at[1])
        wait(rcvz, send_sem.at[4])
    wait(rcvy1, send_sem.at[2])
    wait(snd1.at[:, 0:3], send_sem.at[3])


def solution(mesh):
    def step(images, conv_one, conv_two, mix_weight):
        chunk = (16, 320)
        vmem = functools.partial(pltpu.VMEM, dtype=BF16)
        dma = pltpu.SemaphoreType.DMA
        return pl.pallas_call(
            kernel,
            out_shape=jax.ShapeDtypeStruct((1, *chunk), BF16),
            in_specs=[pl.BlockSpec(memory_space=pl.ANY)] * 4,
            out_specs=pl.BlockSpec(memory_space=pltpu.VMEM),
            scratch_shapes=[
                vmem((2, 80, 1024)),
                vmem((3, 3, 80, 320)),
                vmem((3, 3, 160, 320)),
                vmem((160, 320)),
                vmem((192, 768)),
                vmem((3, 256, 240)),
                vmem((2, NX, 4, *chunk)),
                vmem((2, 4, NX - 1, *chunk)),
                vmem((2, 4, *chunk)),
                vmem((NY - 1, *chunk)),
                vmem((2, NX, 4, *chunk)),
                vmem((2, NC, 16, 160)),
                vmem((2, NC - 1, 16, 160)),
                vmem((2, NC, 16, 160)),
                vmem((2, NX, 4, *chunk)),
                vmem((2, 4, NX - 1, *chunk)),
                vmem((2, 4, *chunk)),
                vmem((NY - 1, *chunk)),
                dma((5,)),
                dma((5,)),
                dma((2, 4)),
                dma,
                dma((NY - 1,)),
                dma((2,)),
                dma((2,)),
                dma((2,)),
                dma((2, 4)),
                dma,
            ],
            compiler_params=pltpu.CompilerParams(
                collective_id=0, has_side_effects=True, vmem_limit_bytes=48 * 2**20
            ),
            name="block",
        )(images, conv_one, conv_two, mix_weight)

    in_specs = (
        P(("section", "dp"), None),
        P(None, None, ("section", "dp"), "chan"),
        P(None, None, ("section", "dp"), "chan"),
        P(("section", "dp"), "chan"),
    )
    out_specs = P("dp", "section", "chan")
    return jax.shard_map(step, mesh=mesh, in_specs=in_specs, out_specs=out_specs, check_vma=False)
```

```python
import functools

import jax
import jax.numpy as jnp
from jax import lax
from jax.experimental import pallas as pl
from jax.experimental.pallas import tpu as pltpu
from jax.sharding import PartitionSpec as P

MESH = pl.DeviceIdType.MESH
BF16 = jnp.bfloat16
F32 = jnp.float32
NX, NY, NZ = 4, 8, 8
CHUNK = (16, 320)
SUBS = 2
IMGS = 4 // SUBS
ZROWS = 32 // SUBS
FAR = (4, 3, 5, 2, 6, 1, 7)


def nt(a, b):
    return lax.dot_general(a, b, (((1,), (1,)), ((), ())), preferred_element_type=F32)


def selection():
    row = lax.broadcasted_iota(jnp.int32, (192, 768), 0)
    col = lax.broadcasted_iota(jnp.int32, (192, 768), 1)
    a, i, j = row >> 6, (row >> 3) & 7, row & 7
    b, place = col >> 8, col & 255
    wanted = (2 * i + a - 1) * 16 + 2 * j + b - 1
    inside = jnp.logical_or(j > 0, b > 0)
    hit = jnp.logical_and(wanted == place, inside)
    return jnp.where(hit, 1.0, 0.0).astype(BF16)


def kernel(
    images, conv_one, conv_two, mix_weight, out,
    maps, w1, w2, wm, sel, lhs, snd1, rcvx1, ybuf1, rcvy1, mine, agbuf, hid, zsnd, rcvz, gat,
    snd3, rcvx3, ybuf3, rcvy3, load_sem, send_sem, swap_sem, rx1, ry1, ay, ax, rz, az, rx3, ry3,
):
    s, c, d = lax.axis_index("section"), lax.axis_index("chan"), lax.axis_index("dp")
    x = d % NX
    y = s * 2 + d // NX
    z = c // 2
    core = c % 2
    par = y % 2
    quarter = y // 2

    def at_x(k, to_core):
        return (s, z * 2 + to_core, (d // NX) * NX + (x + k) % NX)

    def at_y(k):
        to = (y + k) % NY
        return (to // 2, c, (to % 2) * NX + x)

    def at_z(k):
        return (s, ((z + k) % NZ) * 2 + core, d)

    partner = (s, z * 2 + 1 - core, d)

    barrier = pltpu.get_barrier_semaphore()

    def greet(to):
        pl.semaphore_signal(barrier, 1, device_id=to, device_id_type=MESH)

    for k in FAR:
        greet(at_y(k))
        greet(at_z(k))
    for k in (2, 1, 3):
        greet(at_x(k, core))
        greet(at_x(k, 1 - core))
    greet(partner)

    loads = [
        pltpu.make_async_copy(images.at[:, pl.ds(pl.multiple_of((1 - par) * 1024, 1024), 1024)], maps.at[0], load_sem.at[0]),
        pltpu.make_async_copy(conv_one, w1, load_sem.at[2]),
        pltpu.make_async_copy(images.at[:, pl.ds(pl.multiple_of(par * 1024, 1024), 1024)], maps.at[1], load_sem.at[1]),
        pltpu.make_async_copy(conv_two, w2.at[core], load_sem.at[3]),
        pltpu.make_async_copy(mix_weight, wm.at[core], load_sem.at[4]),
    ]
    for copy in loads:
        copy.start()

    def send(src, dst, which, sem, to):
        pltpu.make_async_remote_copy(
            src_ref=src, dst_ref=dst, send_sem=send_sem.at[which], recv_sem=sem, device_id=to, device_id_type=MESH
        ).start()

    def wait(ref, sem):
        pltpu.make_async_copy(ref, ref, sem).wait()

    sel[...] = selection()
    zero = jnp.zeros((80, 256), BF16)
    for g in range(2):
        loads[0 if g == 0 else 2].wait()
        for n in range(4):
            one = maps[g, :, n * 256 : (n + 1) * 256]
            spread = jnp.concatenate(
                [
                    jnp.concatenate([one, zero, zero], 1),
                    jnp.concatenate([zero, one, zero], 1),
                    jnp.concatenate([zero, zero, one], 1),
                ],
                0,
            )
            windows = nt(sel[...], spread).astype(BF16)
            for a in range(3):
                lhs[a, n * 64 : (n + 1) * 64] = windows[a * 64 : (a + 1) * 64]
        if g == 0:
            loads[1].wait()
        total = jnp.zeros((256, 320), F32)
        for a in range(3):
            total = total + jnp.dot(lhs[a], w1[a].reshape(240, 320), preferred_element_type=F32)
        snd1[g] = total.astype(BF16).reshape(4, 4, *CHUNK)
        if g == 0:
            pl.semaphore_wait(barrier, 2 * (NX - 1) + 1 + (NY - 1) + (NZ - 1))
        for r in range(4):
            q = ((y + (4 - g + 2 * r) % NY) % NY) // 2
            for k in (2, 1, 3):
                send(snd1.at[g, (x + k) % NX, q], rcvx1.at[g, r, k - 1], 0, rx1.at[g, r], at_x(k, core))

    loads[3].wait()
    send(w2.at[core], w2.at[core], 5, swap_sem.at[0], partner)
    loads[4].wait()
    send(wm.at[core], wm.at[core], 6, swap_sem.at[1], partner)

    own = None
    for g in range(2):
        for r in range(4):
            k = (4 - g + 2 * r) % NY
            q = ((y + k) % NY) // 2
            wait(rcvx1.at[g, r], rx1.at[g, r])
            total = snd1[g, x, q].astype(F32)
            for other in range(NX - 1):
                total = total + rcvx1[g, r, other].astype(F32)
            if k == 0:
                own = total
            else:
                ybuf1[k - 1] = total.astype(BF16)
                send(ybuf1.at[k - 1], rcvy1.at[k - 1], 1, ry1, at_y(k))
    wait(rcvy1, ry1)
    for k in range(NY - 1):
        own = own + rcvy1[k].astype(F32)
    mine[...] = own.astype(BF16)

    for k in FAR:
        send(mine, agbuf.at[k - 1], 2, ay.at[k - 1], at_y(k))
    sub = x // IMGS
    for k in (0, 1, 7, 2, 6, 3, 5, 4):
        origin = (y - k + NY) % NY
        q = origin // 2
        to_core = 1 - origin % 2
        here = hid.at[core, x, q]
        if k == 0:
            src = mine
        else:
            src = agbuf.at[k - 1]
            wait(src, ay.at[k - 1])
        for kx in (2, 1, 3):
            send(src, here, 3, ax.at[sub], at_x(kx, to_core))

        @pl.when(to_core == core)
        def _():
            pltpu.make_async_copy(src, here, ax.at[sub]).start()

        @pl.when(to_core != core)
        def _():
            send(src, here, 3, ax.at[sub], partner)

    wait(w2.at[0], swap_sem.at[0])
    for t in range(SUBS):
        wait(hid.at[:, t * IMGS : (t + 1) * IMGS], ax.at[t])
        rows = IMGS * 64
        parts = [jnp.zeros((rows, 160), F32) for _ in range(3)]
        place = lax.broadcasted_iota(jnp.int32, (rows // 8, 8, 320), 1)
        for j in range(2):
            block = hid[j, t * IMGS : (t + 1) * IMGS].reshape(rows, 320)
            rect = jnp.maximum(block.astype(F32), 0.0).reshape(rows // 8, 8, 320)
            left = jnp.where(place == 0, 0.0, pltpu.roll(rect, 1, 1))
            right = jnp.where(place == 7, 0.0, pltpu.roll(rect, 7, 1))
            shifted = [v.reshape(rows, 320).astype(BF16) for v in (left, rect, right)]
            for a in range(3):
                for b in range(3):
                    parts[a] = parts[a] + nt(shifted[b], w2[j, a, b])
        parts = [v.reshape(IMGS, 64, 160) for v in parts]
        gap = jnp.zeros((IMGS, 8, 160), F32)
        inner = (
            parts[1]
            + jnp.concatenate([gap, parts[0][:, :56]], 1)
            + jnp.concatenate([parts[2][:, 8:], gap], 1)
        )
        zsnd[t] = inner.astype(BF16).reshape(NZ, ZROWS, 160)
        for k in FAR:
            send(zsnd.at[t, (z + k) % NZ], rcvz.at[t, k - 1], 4, rz.at[t], at_z(k))

    for t in range(SUBS):
        wait(rcvz.at[t], rz.at[t])
        total = zsnd[t, z].astype(F32)
        for k in range(NZ - 1):
            total = total + rcvz[t, k].astype(F32)
        gat[t, z] = jnp.maximum(total, 0.0).astype(BF16)
        for k in FAR:
            send(gat.at[t, z], gat.at[t, z], 4, az.at[t], at_z(k))

    wait(wm.at[0], swap_sem.at[1])
    for t in range(SUBS):
        wait(gat.at[t, 0 : NZ - 1], az.at[t])
        gated = gat[t].reshape(IMGS * 64, 160)
        for j in range(2):
            mixed = jnp.dot(gated, wm[j], preferred_element_type=F32).astype(BF16)
            snd3[j, t * IMGS : (t + 1) * IMGS] = mixed.reshape(IMGS, 4, *CHUNK)
    apart = (core + y) % 2
    for r in range(4):
        k = (4 - apart + 2 * r) % NY
        q = ((y + k) % NY) // 2
        for kx in (2, 1, 3):
            for j in range(2):
                send(snd3.at[j, (x + kx) % NX, q], rcvx3.at[k, kx], 0, rx3.at[k], at_x(kx, j))
        send(snd3.at[1 - core, x, q], rcvx3.at[k, 0], 0, rx3.at[k], partner)
        pltpu.make_async_copy(snd3.at[core, x, q], rcvx3.at[k, 0], rx3.at[k]).start()
    own = None
    for k in (*FAR, 0):
        wait(rcvx3.at[k], rx3.at[k])
        total = rcvx3[k, 0].astype(F32)
        for other in range(1, NX):
            total = total + rcvx3[k, other].astype(F32)
        if k == 0:
            own = total
        else:
            ybuf3[k - 1] = total.astype(BF16)
            send(ybuf3.at[k - 1], rcvy3.at[k - 1], 1, ry3, at_y(k))
    skip = agbuf[6 * (1 - par)]
    own = own + skip.astype(F32)
    wait(rcvy3, ry3)
    for k in range(NY - 1):
        own = own + rcvy3[k].astype(F32)
    out[0] = own.astype(BF16)

    for _ in range(4):
        wait(agbuf, send_sem.at[3])
    for _ in range(2):
        wait(snd1.at[:, 0:3], send_sem.at[0])
        wait(rcvy1, send_sem.at[1])
        wait(rcvz, send_sem.at[4])
    wait(hid.at[0, 0], send_sem.at[0])
    wait(agbuf, send_sem.at[2])
    wait(w2.at[0], send_sem.at[5])
    wait(wm.at[0], send_sem.at[6])


def solution(mesh):
    def step(images, conv_one, conv_two, mix_weight):
        vmem = functools.partial(pltpu.VMEM, dtype=BF16)
        dma = pltpu.SemaphoreType.DMA
        return pl.pallas_call(
            kernel,
            out_shape=jax.ShapeDtypeStruct((1, *CHUNK), BF16),
            in_specs=[pl.BlockSpec(memory_space=pl.ANY)] * 4,
            out_specs=pl.BlockSpec(memory_space=pltpu.VMEM),
            scratch_shapes=[
                vmem((2, 80, 1024)),
                vmem((3, 3, 80, 320)),
                vmem((2, 3, 3, 160, 320)),
                vmem((2, 160, 320)),
                vmem((192, 768)),
                vmem((3, 256, 240)),
                vmem((2, NX, 4, *CHUNK)),
                vmem((2, 4, NX - 1, *CHUNK)),
                vmem((NY - 1, *CHUNK)),
                vmem((NY - 1, *CHUNK)),
                vmem(CHUNK),
                vmem((NY - 1, *CHUNK)),
                vmem((2, NX, 4, *CHUNK)),
                vmem((SUBS, NZ, ZROWS, 160)),
                vmem((SUBS, NZ - 1, ZROWS, 160)),
                vmem((SUBS, NZ, ZROWS, 160)),
                vmem((2, NX, 4, *CHUNK)),
                vmem((NY, NX, *CHUNK)),
                vmem((NY - 1, *CHUNK)),
                vmem((NY - 1, *CHUNK)),
                dma((5,)),
                dma((7,)),
                dma((2,)),
                dma((2, 4)),
                dma,
                dma((NY - 1,)),
                dma((SUBS,)),
                dma((SUBS,)),
                dma((SUBS,)),
                dma((NY,)),
                dma,
            ],
            compiler_params=pltpu.CompilerParams(
                collective_id=0, has_side_effects=True, vmem_limit_bytes=60 * 2**20
            ),
            name="block",
        )(images, conv_one, conv_two, mix_weight)

    in_specs = (
        P(("section", "dp"), None),
        P(None, None, ("section", "dp"), "chan"),
        P(None, None, ("section", "dp"), "chan"),
        P(("section", "dp"), "chan"),
    )
    out_specs = P("dp", "section", "chan")
    return jax.shard_map(step, mesh=mesh, in_specs=in_specs, out_specs=out_specs, check_vma=False)
```

```python
import functools

import jax
import jax.numpy as jnp
from jax import lax
from jax.experimental import pallas as pl
from jax.experimental.pallas import tpu as pltpu
from jax.sharding import PartitionSpec as P

MESH = pl.DeviceIdType.MESH
BF16 = jnp.bfloat16
F32 = jnp.float32
NX, NY, NZ = 4, 8, 8
CHUNK = (16, 320)
SUBS = 2
IMGS = 4 // SUBS
ZROWS = 32 // SUBS
FAR = (4, 3, 5, 2, 6, 1, 7)


def nt(a, b):
    return lax.dot_general(a, b, (((1,), (1,)), ((), ())), preferred_element_type=F32)


def selection():
    row = lax.broadcasted_iota(jnp.int32, (192, 768), 0)
    col = lax.broadcasted_iota(jnp.int32, (192, 768), 1)
    a, i, j = row >> 6, (row >> 3) & 7, row & 7
    b, place = col >> 8, col & 255
    wanted = (2 * i + a - 1) * 16 + 2 * j + b - 1
    inside = jnp.logical_or(j > 0, b > 0)
    hit = jnp.logical_and(wanted == place, inside)
    return jnp.where(hit, 1.0, 0.0).astype(BF16)


def kernel(
    images, conv_one, conv_two, mix_weight, out,
    maps, w1, w2, wm, sel, lhs, snd1, rcvx1, ybuf1, rcvy1, mine, agbuf, hid, zsnd, rcvz, gat,
    snd3, rcvx3, ybuf3, rcvy3, load_sem, send_sem, swap_sem, rx1, ry1, ay, ax, rz, az, rx3, ry3,
):
    s, c, d = lax.axis_index("section"), lax.axis_index("chan"), lax.axis_index("dp")
    x = d % NX
    y = s * 2 + d // NX
    z = c // 2
    core = c % 2
    par = y % 2
    quarter = y // 2

    def at_x(k, to_core):
        return (s, z * 2 + to_core, (d // NX) * NX + (x + k) % NX)

    def at_y(k):
        to = (y + k) % NY
        return (to // 2, c, (to % 2) * NX + x)

    def at_z(k):
        return (s, ((z + k) % NZ) * 2 + core, d)

    partner = (s, z * 2 + 1 - core, d)

    barrier = pltpu.get_barrier_semaphore()

    def greet(to):
        pl.semaphore_signal(barrier, 1, device_id=to, device_id_type=MESH)

    for k in FAR:
        greet(at_y(k))
        greet(at_z(k))
    for k in (2, 1, 3):
        greet(at_x(k, core))
        greet(at_x(k, 1 - core))
    greet(partner)

    loads = [
        pltpu.make_async_copy(images.at[:, pl.ds(pl.multiple_of((1 - par) * 1024, 1024), 1024)], maps.at[0], load_sem.at[0]),
        pltpu.make_async_copy(conv_one, w1, load_sem.at[2]),
        pltpu.make_async_copy(images.at[:, pl.ds(pl.multiple_of(par * 1024, 1024), 1024)], maps.at[1], load_sem.at[1]),
        pltpu.make_async_copy(conv_two, w2.at[core], load_sem.at[3]),
        pltpu.make_async_copy(mix_weight, wm.at[core], load_sem.at[4]),
    ]
    for copy in loads:
        copy.start()

    def send(src, dst, which, sem, to):
        pltpu.make_async_remote_copy(
            src_ref=src, dst_ref=dst, send_sem=send_sem.at[which], recv_sem=sem, device_id=to, device_id_type=MESH
        ).start()

    def wait(ref, sem):
        pltpu.make_async_copy(ref, ref, sem).wait()

    sel[...] = selection()
    zero = jnp.zeros((80, 256), BF16)
    for g in range(2):
        loads[0 if g == 0 else 2].wait()
        for n in range(4):
            one = maps[g, :, n * 256 : (n + 1) * 256]
            spread = jnp.concatenate(
                [
                    jnp.concatenate([one, zero, zero], 1),
                    jnp.concatenate([zero, one, zero], 1),
                    jnp.concatenate([zero, zero, one], 1),
                ],
                0,
            )
            windows = nt(sel[...], spread).astype(BF16)
            for a in range(3):
                lhs[a, n * 64 : (n + 1) * 64] = windows[a * 64 : (a + 1) * 64]
        if g == 0:
            loads[1].wait()
        total = jnp.zeros((256, 320), F32)
        for a in range(3):
            total = total + jnp.dot(lhs[a], w1[a].reshape(240, 320), preferred_element_type=F32)
        snd1[g] = total.astype(BF16).reshape(4, 4, *CHUNK)
        if g == 0:
            pl.semaphore_wait(barrier, 2 * (NX - 1) + 1 + (NY - 1) + (NZ - 1))
        for r in (0, 1, 3, 2):
            q = ((y + (4 - g + 2 * r) % NY) % NY) // 2
            for k in (2, 1, 3):
                send(snd1.at[g, (x + k) % NX, q], rcvx1.at[g, r, k - 1], 0, rx1.at[g, r], at_x(k, core))

    loads[3].wait()
    send(w2.at[core], w2.at[core], 5, swap_sem.at[0], partner)
    loads[4].wait()
    send(wm.at[core], wm.at[core], 6, swap_sem.at[1], partner)

    own = None
    for g in range(2):
        for r in (0, 1, 3, 2):
            k = (4 - g + 2 * r) % NY
            q = ((y + k) % NY) // 2
            wait(rcvx1.at[g, r], rx1.at[g, r])
            total = snd1[g, x, q].astype(F32)
            for other in range(NX - 1):
                total = total + rcvx1[g, r, other].astype(F32)
            if k == 0:
                own = total
            else:
                ybuf1[k - 1] = total.astype(BF16)
                send(ybuf1.at[k - 1], rcvy1.at[k - 1], 1, ry1, at_y(k))
    wait(rcvy1, ry1)
    for k in range(NY - 1):
        own = own + rcvy1[k].astype(F32)
    mine[...] = own.astype(BF16)

    for k in FAR:
        send(mine, agbuf.at[k - 1], 2, ay.at[k - 1], at_y(k))
    sub = x // IMGS
    for k in (0, 1, 7, 2, 6, 3, 5, 4):
        origin = (y - k + NY) % NY
        q = origin // 2
        to_core = 1 - origin % 2
        here = hid.at[core, x, q]
        if k == 0:
            src = mine
        else:
            src = agbuf.at[k - 1]
            wait(src, ay.at[k - 1])
        for kx in (2, 1, 3):
            send(src, here, 3, ax.at[sub], at_x(kx, to_core))

        @pl.when(to_core == core)
        def _():
            pltpu.make_async_copy(src, here, ax.at[sub]).start()

        @pl.when(to_core != core)
        def _():
            send(src, here, 3, ax.at[sub], partner)

    wait(w2.at[0], swap_sem.at[0])
    for t in range(SUBS):
        wait(hid.at[:, t * IMGS : (t + 1) * IMGS], ax.at[t])
        rows = IMGS * 64
        parts = [jnp.zeros((rows, 160), F32) for _ in range(3)]
        place = lax.broadcasted_iota(jnp.int32, (rows // 8, 8, 320), 1)
        for j in range(2):
            block = hid[j, t * IMGS : (t + 1) * IMGS].reshape(rows, 320)
            rect = jnp.maximum(block.astype(F32), 0.0).reshape(rows // 8, 8, 320)
            left = jnp.where(place == 0, 0.0, pltpu.roll(rect, 1, 1))
            right = jnp.where(place == 7, 0.0, pltpu.roll(rect, 7, 1))
            shifted = [v.reshape(rows, 320).astype(BF16) for v in (left, rect, right)]
            for a in range(3):
                for b in range(3):
                    parts[a] = parts[a] + nt(shifted[b], w2[j, a, b])
        parts = [v.reshape(IMGS, 64, 160) for v in parts]
        gap = jnp.zeros((IMGS, 8, 160), F32)
        inner = (
            parts[1]
            + jnp.concatenate([gap, parts[0][:, :56]], 1)
            + jnp.concatenate([parts[2][:, 8:], gap], 1)
        )
        zsnd[t] = inner.astype(BF16).reshape(NZ, ZROWS, 160)
        for k in FAR:
            send(zsnd.at[t, (z + k) % NZ], rcvz.at[t, k - 1], 4, rz.at[t], at_z(k))

    for t in range(SUBS):
        wait(rcvz.at[t], rz.at[t])
        total = zsnd[t, z].astype(F32)
        for k in range(NZ - 1):
            total = total + rcvz[t, k].astype(F32)
        gat[t, z] = jnp.maximum(total, 0.0).astype(BF16)
        for k in FAR:
            send(gat.at[t, z], gat.at[t, z], 4, az.at[t], at_z(k))

    apart = (core + y) % 2
    wait(wm.at[0], swap_sem.at[1])
    for t in range(SUBS):
        wait(gat.at[t, 0 : NZ - 1], az.at[t])
        gated = gat[t].reshape(IMGS * 64, 160)
        for j in range(2):
            mixed = jnp.dot(gated, wm[j], preferred_element_type=F32).astype(BF16)
            snd3[j, t * IMGS : (t + 1) * IMGS] = mixed.reshape(IMGS, 4, *CHUNK)
        for r in (0, 1, 3, 2):
            k = (4 - apart + 2 * r) % NY
            q = ((y + k) % NY) // 2
            for to_x in range(t * IMGS, (t + 1) * IMGS):

                @pl.when(x != to_x)
                def _():
                    kx = (to_x - x + NX) % NX
                    for j in range(2):
                        send(snd3.at[j, to_x, q], rcvx3.at[k, kx], 0, rx3.at[k], at_x(kx, j))

                @pl.when(x == to_x)
                def _():
                    send(snd3.at[1 - core, to_x, q], rcvx3.at[k, 0], 0, rx3.at[k], partner)
                    pltpu.make_async_copy(snd3.at[core, to_x, q], rcvx3.at[k, 0], rx3.at[k]).start()

    own = None
    for k in (4, 3, 6, 5, 2, 1, 7, 0):
        wait(rcvx3.at[k], rx3.at[k])
        total = rcvx3[k, 0].astype(F32)
        for other in range(1, NX):
            total = total + rcvx3[k, other].astype(F32)
        if k == 0:
            own = total
        else:
            ybuf3[k - 1] = total.astype(BF16)
            send(ybuf3.at[k - 1], rcvy3.at[k - 1], 1, ry3, at_y(k))
    skip = agbuf[6 * (1 - par)]
    own = own + skip.astype(F32)
    wait(rcvy3, ry3)
    for k in range(NY - 1):
        own = own + rcvy3[k].astype(F32)
    out[0] = own.astype(BF16)

    for _ in range(4):
        wait(agbuf, send_sem.at[3])
    for _ in range(2):
        wait(snd1.at[:, 0:3], send_sem.at[0])
        wait(rcvy1, send_sem.at[1])
        wait(rcvz, send_sem.at[4])
    wait(hid.at[0, 0], send_sem.at[0])
    wait(agbuf, send_sem.at[2])
    wait(w2.at[0], send_sem.at[5])
    wait(wm.at[0], send_sem.at[6])


def solution(mesh):
    def step(images, conv_one, conv_two, mix_weight):
        vmem = functools.partial(pltpu.VMEM, dtype=BF16)
        dma = pltpu.SemaphoreType.DMA
        return pl.pallas_call(
            kernel,
            out_shape=jax.ShapeDtypeStruct((1, *CHUNK), BF16),
            in_specs=[pl.BlockSpec(memory_space=pl.ANY)] * 4,
            out_specs=pl.BlockSpec(memory_space=pltpu.VMEM),
            scratch_shapes=[
                vmem((2, 80, 1024)),
                vmem((3, 3, 80, 320)),
                vmem((2, 3, 3, 160, 320)),
                vmem((2, 160, 320)),
                vmem((192, 768)),
                vmem((3, 256, 240)),
                vmem((2, NX, 4, *CHUNK)),
                vmem((2, 4, NX - 1, *CHUNK)),
                vmem((NY - 1, *CHUNK)),
                vmem((NY - 1, *CHUNK)),
                vmem(CHUNK),
                vmem((NY - 1, *CHUNK)),
                vmem((2, NX, 4, *CHUNK)),
                vmem((SUBS, NZ, ZROWS, 160)),
                vmem((SUBS, NZ - 1, ZROWS, 160)),
                vmem((SUBS, NZ, ZROWS, 160)),
                vmem((2, NX, 4, *CHUNK)),
                vmem((NY, NX, *CHUNK)),
                vmem((NY - 1, *CHUNK)),
                vmem((NY - 1, *CHUNK)),
                dma((5,)),
                dma((7,)),
                dma((2,)),
                dma((2, 4)),
                dma,
                dma((NY - 1,)),
                dma((SUBS,)),
                dma((SUBS,)),
                dma((SUBS,)),
                dma((NY,)),
                dma,
            ],
            compiler_params=pltpu.CompilerParams(
                collective_id=0, has_side_effects=True, vmem_limit_bytes=60 * 2**20
            ),
            name="block",
        )(images, conv_one, conv_two, mix_weight)

    in_specs = (
        P(("section", "dp"), None),
        P(None, None, ("section", "dp"), "chan"),
        P(None, None, ("section", "dp"), "chan"),
        P(("section", "dp"), "chan"),
    )
    out_specs = P("dp", "section", "chan")
    return jax.shard_map(step, mesh=mesh, in_specs=in_specs, out_specs=out_specs, check_vma=False)
```

```python
import functools

import jax
import jax.numpy as jnp
from jax import lax
from jax.experimental import pallas as pl
from jax.experimental.pallas import tpu as pltpu
from jax.sharding import PartitionSpec as P

MESH = pl.DeviceIdType.MESH
BF16 = jnp.bfloat16
F32 = jnp.float32
NX, NY, NZ = 4, 8, 8
CHUNK = (16, 320)
SUBS = 2
IMGS = 4 // SUBS
ZROWS = 32 // SUBS
FAR = (4, 3, 5, 2, 6, 1, 7)


def nt(a, b):
    return lax.dot_general(a, b, (((1,), (1,)), ((), ())), preferred_element_type=F32)


def selection():
    row = lax.broadcasted_iota(jnp.int32, (192, 768), 0)
    col = lax.broadcasted_iota(jnp.int32, (192, 768), 1)
    a, i, j = row >> 6, (row >> 3) & 7, row & 7
    b, place = col >> 8, col & 255
    wanted = (2 * i + a - 1) * 16 + 2 * j + b - 1
    inside = jnp.logical_or(j > 0, b > 0)
    hit = jnp.logical_and(wanted == place, inside)
    return jnp.where(hit, 1.0, 0.0).astype(BF16)


def kernel(
    images, conv_one, conv_two, mix_weight, out,
    maps, w1, w2, wm, sel, lhs, snd1, rcvx1, ybuf1, rcvy1, mine, agbuf, hid, zsnd, rcvz, gat,
    snd3, rcvx3, ybuf3, rcvy3, load_sem, send_sem, swap_sem, rx1, ry1, ay, ax, rz, az, rx3, ry3,
):
    s, c, d = lax.axis_index("section"), lax.axis_index("chan"), lax.axis_index("dp")
    x = d % NX
    y = s * 2 + d // NX
    z = c // 2
    core = c % 2
    par = y % 2
    quarter = y // 2

    def at_x(k, to_core):
        return (s, z * 2 + to_core, (d // NX) * NX + (x + k) % NX)

    def at_y(k):
        to = (y + k) % NY
        return (to // 2, c, (to % 2) * NX + x)

    def at_z(k):
        return (s, ((z + k) % NZ) * 2 + core, d)

    partner = (s, z * 2 + 1 - core, d)

    barrier = pltpu.get_barrier_semaphore()

    def greet(to):
        pl.semaphore_signal(barrier, 1, device_id=to, device_id_type=MESH)

    for k in FAR:
        greet(at_y(k))
        greet(at_z(k))
    for k in (2, 1, 3):
        greet(at_x(k, core))
        greet(at_x(k, 1 - core))
    greet(partner)

    loads = [
        pltpu.make_async_copy(images.at[:, pl.ds(pl.multiple_of((1 - par) * 1024, 1024), 1024)], maps.at[0], load_sem.at[0]),
        pltpu.make_async_copy(conv_one, w1, load_sem.at[2]),
        pltpu.make_async_copy(images.at[:, pl.ds(pl.multiple_of(par * 1024, 1024), 1024)], maps.at[1], load_sem.at[1]),
        pltpu.make_async_copy(conv_two, w2.at[core], load_sem.at[3]),
        pltpu.make_async_copy(mix_weight, wm.at[core], load_sem.at[4]),
    ]
    for copy in loads:
        copy.start()

    def send(src, dst, which, sem, to):
        pltpu.make_async_remote_copy(
            src_ref=src, dst_ref=dst, send_sem=send_sem.at[which], recv_sem=sem, device_id=to, device_id_type=MESH
        ).start()

    def wait(ref, sem):
        pltpu.make_async_copy(ref, ref, sem).wait()

    sel[...] = selection()
    zero = jnp.zeros((80, 256), BF16)
    for g in range(2):
        loads[0 if g == 0 else 2].wait()
        for n in range(4):
            one = maps[g, :, n * 256 : (n + 1) * 256]
            spread = jnp.concatenate(
                [
                    jnp.concatenate([one, zero, zero], 1),
                    jnp.concatenate([zero, one, zero], 1),
                    jnp.concatenate([zero, zero, one], 1),
                ],
                0,
            )
            windows = nt(sel[...], spread).astype(BF16)
            for a in range(3):
                lhs[a, n * 64 : (n + 1) * 64] = windows[a * 64 : (a + 1) * 64]
        if g == 0:
            loads[1].wait()
        total = jnp.zeros((256, 320), F32)
        for a in range(3):
            total = total + jnp.dot(lhs[a], w1[a].reshape(240, 320), preferred_element_type=F32)
        snd1[g] = total.astype(BF16).reshape(4, 4, *CHUNK)
        if g == 0:
            pl.semaphore_wait(barrier, 2 * (NX - 1) + 1 + (NY - 1) + (NZ - 1))
        for r in (0, 1, 3, 2):
            q = ((y + (4 - g + 2 * r) % NY) % NY) // 2
            for k in (2, 1, 3):
                send(snd1.at[g, (x + k) % NX, q], rcvx1.at[g, r, k - 1], 0, rx1.at[g, r], at_x(k, core))

    loads[3].wait()
    send(w2.at[core], w2.at[core], 5, swap_sem.at[0], partner)
    loads[4].wait()
    send(wm.at[core], wm.at[core], 6, swap_sem.at[1], partner)

    own = None
    for g in range(2):
        for r in (0, 1, 3, 2):
            k = (4 - g + 2 * r) % NY
            q = ((y + k) % NY) // 2
            wait(rcvx1.at[g, r], rx1.at[g, r])
            total = snd1[g, x, q].astype(F32)
            for other in range(NX - 1):
                total = total + rcvx1[g, r, other].astype(F32)
            if k == 0:
                own = total
            else:
                ybuf1[k - 1] = total.astype(BF16)
                send(ybuf1.at[k - 1], rcvy1.at[k - 1], 1, ry1, at_y(k))
    wait(rcvy1, ry1)
    for k in range(NY - 1):
        own = own + rcvy1[k].astype(F32)
    mine[...] = own.astype(BF16)

    for k in FAR:
        send(mine, agbuf.at[k - 1], 2, ay.at[k - 1], at_y(k))
    sub = x // IMGS
    for k in (0, 1, 7, 2, 6, 3, 5, 4):
        origin = (y - k + NY) % NY
        q = origin // 2
        to_core = 1 - origin % 2
        here = hid.at[core, x, q]
        if k == 0:
            src = mine
        else:
            src = agbuf.at[k - 1]
            wait(src, ay.at[k - 1])
        for kx in (2, 1, 3):
            send(src, here, 3, ax.at[sub], at_x(kx, to_core))

        @pl.when(to_core == core)
        def _():
            pltpu.make_async_copy(src, here, ax.at[sub]).start()

        @pl.when(to_core != core)
        def _():
            send(src, here, 3, ax.at[sub], partner)

    wait(w2.at[0], swap_sem.at[0])
    for t in range(SUBS):
        wait(hid.at[:, t * IMGS : (t + 1) * IMGS], ax.at[t])
        rows = IMGS * 64
        parts = [jnp.zeros((rows, 160), F32) for _ in range(3)]
        place = lax.broadcasted_iota(jnp.int32, (rows // 8, 8, 320), 1)
        for j in range(2):
            block = hid[j, t * IMGS : (t + 1) * IMGS].reshape(rows, 320)
            rect = jnp.maximum(block.astype(F32), 0.0).reshape(rows // 8, 8, 320)
            left = jnp.where(place == 0, 0.0, pltpu.roll(rect, 1, 1))
            right = jnp.where(place == 7, 0.0, pltpu.roll(rect, 7, 1))
            shifted = [v.reshape(rows, 320).astype(BF16) for v in (left, rect, right)]
            for a in range(3):
                for b in range(3):
                    parts[a] = parts[a] + nt(shifted[b], w2[j, a, b])
        parts = [v.reshape(IMGS, 64, 160) for v in parts]
        gap = jnp.zeros((IMGS, 8, 160), F32)
        inner = (
            parts[1]
            + jnp.concatenate([gap, parts[0][:, :56]], 1)
            + jnp.concatenate([parts[2][:, 8:], gap], 1)
        )
        zsnd[t] = inner.astype(BF16).reshape(NZ, ZROWS, 160)
        for k in FAR:
            send(zsnd.at[t, (z + k) % NZ], rcvz.at[t, k - 1], 4, rz.at[t], at_z(k))

    for t in range(SUBS):
        wait(rcvz.at[t], rz.at[t])
        total = zsnd[t, z].astype(F32)
        for k in range(NZ - 1):
            total = total + rcvz[t, k].astype(F32)
        gat[t, z] = jnp.maximum(total, 0.0).astype(BF16)
        for to_z in (0, 1, 2, 3, 7, 6, 5, 4):

            @pl.when(to_z != z)
            def _():
                send(gat.at[t, z], gat.at[t, z], 4, az.at[t], at_z(to_z - z + NZ))

    apart = (core + y) % 2
    wait(wm.at[0], swap_sem.at[1])
    for t in range(SUBS):
        wait(gat.at[t, 0 : NZ - 1], az.at[t])
        gated = gat[t].reshape(IMGS * 64, 160)
        for j in range(2):
            mixed = jnp.dot(gated, wm[j], preferred_element_type=F32).astype(BF16)
            snd3[j, t * IMGS : (t + 1) * IMGS] = mixed.reshape(IMGS, 4, *CHUNK)
        for r in (0, 1, 3, 2):
            k = (4 - apart + 2 * r) % NY
            q = ((y + k) % NY) // 2
            for to_x in range(t * IMGS, (t + 1) * IMGS):

                @pl.when(x != to_x)
                def _():
                    kx = (to_x - x + NX) % NX
                    for j in range(2):
                        send(snd3.at[j, to_x, q], rcvx3.at[k, kx], 0, rx3.at[k], at_x(kx, j))

                @pl.when(x == to_x)
                def _():
                    send(snd3.at[1 - core, to_x, q], rcvx3.at[k, 0], 0, rx3.at[k], partner)
                    pltpu.make_async_copy(snd3.at[core, to_x, q], rcvx3.at[k, 0], rx3.at[k]).start()

    own = None
    for k in (4, 3, 6, 5, 2, 1, 7, 0):
        wait(rcvx3.at[k], rx3.at[k])
        total = rcvx3[k, 0].astype(F32)
        for other in range(1, NX):
            total = total + rcvx3[k, other].astype(F32)
        if k == 0:
            own = total
        else:
            ybuf3[k - 1] = total.astype(BF16)
            send(ybuf3.at[k - 1], rcvy3.at[k - 1], 1, ry3, at_y(k))
    skip = agbuf[6 * (1 - par)]
    own = own + skip.astype(F32)
    wait(rcvy3, ry3)
    for k in range(NY - 1):
        own = own + rcvy3[k].astype(F32)
    out[0] = own.astype(BF16)

    for _ in range(4):
        wait(agbuf, send_sem.at[3])
    for _ in range(2):
        wait(snd1.at[:, 0:3], send_sem.at[0])
        wait(rcvy1, send_sem.at[1])
        wait(rcvz, send_sem.at[4])
    wait(hid.at[0, 0], send_sem.at[0])
    wait(agbuf, send_sem.at[2])
    wait(w2.at[0], send_sem.at[5])
    wait(wm.at[0], send_sem.at[6])


def solution(mesh):
    def step(images, conv_one, conv_two, mix_weight):
        vmem = functools.partial(pltpu.VMEM, dtype=BF16)
        dma = pltpu.SemaphoreType.DMA
        return pl.pallas_call(
            kernel,
            out_shape=jax.ShapeDtypeStruct((1, *CHUNK), BF16),
            in_specs=[pl.BlockSpec(memory_space=pl.ANY)] * 4,
            out_specs=pl.BlockSpec(memory_space=pltpu.VMEM),
            scratch_shapes=[
                vmem((2, 80, 1024)),
                vmem((3, 3, 80, 320)),
                vmem((2, 3, 3, 160, 320)),
                vmem((2, 160, 320)),
                vmem((192, 768)),
                vmem((3, 256, 240)),
                vmem((2, NX, 4, *CHUNK)),
                vmem((2, 4, NX - 1, *CHUNK)),
                vmem((NY - 1, *CHUNK)),
                vmem((NY - 1, *CHUNK)),
                vmem(CHUNK),
                vmem((NY - 1, *CHUNK)),
                vmem((2, NX, 4, *CHUNK)),
                vmem((SUBS, NZ, ZROWS, 160)),
                vmem((SUBS, NZ - 1, ZROWS, 160)),
                vmem((SUBS, NZ, ZROWS, 160)),
                vmem((2, NX, 4, *CHUNK)),
                vmem((NY, NX, *CHUNK)),
                vmem((NY - 1, *CHUNK)),
                vmem((NY - 1, *CHUNK)),
                dma((5,)),
                dma((7,)),
                dma((2,)),
                dma((2, 4)),
                dma,
                dma((NY - 1,)),
                dma((SUBS,)),
                dma((SUBS,)),
                dma((SUBS,)),
                dma((NY,)),
                dma,
            ],
            compiler_params=pltpu.CompilerParams(
                collective_id=0, has_side_effects=True, vmem_limit_bytes=60 * 2**20
            ),
            name="block",
        )(images, conv_one, conv_two, mix_weight)

    in_specs = (
        P(("section", "dp"), None),
        P(None, None, ("section", "dp"), "chan"),
        P(None, None, ("section", "dp"), "chan"),
        P(("section", "dp"), "chan"),
    )
    out_specs = P("dp", "section", "chan")
    return jax.shard_map(step, mesh=mesh, in_specs=in_specs, out_specs=out_specs, check_vma=False)
```

```python
import functools

import jax
import jax.numpy as jnp
from jax import lax
from jax.experimental import pallas as pl
from jax.experimental.pallas import tpu as pltpu
from jax.sharding import PartitionSpec as P

MESH = pl.DeviceIdType.MESH
BF16 = jnp.bfloat16
F32 = jnp.float32
NX, NY, NZ = 4, 8, 8
CHUNK = (16, 320)
SUBS = 2
IMGS = 4 // SUBS
ZROWS = 32 // SUBS
FAR = (4, 3, 5, 2, 6, 1, 7)


def nt(a, b):
    return lax.dot_general(a, b, (((1,), (1,)), ((), ())), preferred_element_type=F32)


def selection():
    row = lax.broadcasted_iota(jnp.int32, (192, 768), 0)
    col = lax.broadcasted_iota(jnp.int32, (192, 768), 1)
    a, i, j = row >> 6, (row >> 3) & 7, row & 7
    b, place = col >> 8, col & 255
    wanted = (2 * i + a - 1) * 16 + 2 * j + b - 1
    inside = jnp.logical_or(j > 0, b > 0)
    hit = jnp.logical_and(wanted == place, inside)
    return jnp.where(hit, 1.0, 0.0).astype(BF16)


def kernel(
    images, conv_one, conv_two, mix_weight, out,
    maps, w1, w2, wm, sel, lhs, snd1, rcvx1, ybuf1, rcvy1, mine, agbuf, hid, zsnd, rcvz, gat,
    snd3, rcvx3, ybuf3, rcvy3, load_sem, send_sem, swap_sem, rx1, ry1, ay, ax, rz, az, rx3, ry3,
):
    s, c, d = lax.axis_index("section"), lax.axis_index("chan"), lax.axis_index("dp")
    x = d % NX
    y = s * 2 + d // NX
    z = c // 2
    core = c % 2
    par = y % 2
    quarter = y // 2

    def at_x(k, to_core):
        return (s, z * 2 + to_core, (d // NX) * NX + (x + k) % NX)

    def at_y(k):
        to = (y + k) % NY
        return (to // 2, c, (to % 2) * NX + x)

    def at_z(k):
        return (s, ((z + k) % NZ) * 2 + core, d)

    partner = (s, z * 2 + 1 - core, d)

    barrier = pltpu.get_barrier_semaphore()

    def greet(to):
        pl.semaphore_signal(barrier, 1, device_id=to, device_id_type=MESH)

    for k in FAR:
        greet(at_y(k))
    for k in (2, 1, 3):
        greet(at_x(k, core))
        greet(at_x(k, 1 - core))
    greet(partner)
    for k in FAR:
        greet(at_z(k))

    loads = [
        pltpu.make_async_copy(images.at[:, pl.ds(pl.multiple_of((1 - par) * 1024, 1024), 1024)], maps.at[0], load_sem.at[0]),
        pltpu.make_async_copy(conv_one, w1, load_sem.at[2]),
        pltpu.make_async_copy(images.at[:, pl.ds(pl.multiple_of(par * 1024, 1024), 1024)], maps.at[1], load_sem.at[1]),
        pltpu.make_async_copy(conv_two, w2.at[core], load_sem.at[3]),
        pltpu.make_async_copy(mix_weight, wm.at[core], load_sem.at[4]),
    ]
    for copy in loads:
        copy.start()

    def send(src, dst, which, sem, to):
        pltpu.make_async_remote_copy(
            src_ref=src, dst_ref=dst, send_sem=send_sem.at[which], recv_sem=sem, device_id=to, device_id_type=MESH
        ).start()

    def wait(ref, sem):
        pltpu.make_async_copy(ref, ref, sem).wait()

    sel[...] = selection()
    zero = jnp.zeros((80, 256), BF16)
    for g in range(2):
        loads[0 if g == 0 else 2].wait()
        for n in range(4):
            one = maps[g, :, n * 256 : (n + 1) * 256]
            spread = jnp.concatenate(
                [
                    jnp.concatenate([one, zero, zero], 1),
                    jnp.concatenate([zero, one, zero], 1),
                    jnp.concatenate([zero, zero, one], 1),
                ],
                0,
            )
            windows = nt(sel[...], spread).astype(BF16)
            for a in range(3):
                lhs[a, n * 64 : (n + 1) * 64] = windows[a * 64 : (a + 1) * 64]
        if g == 0:
            loads[1].wait()
        total = jnp.zeros((256, 320), F32)
        for a in range(3):
            total = total + jnp.dot(lhs[a], w1[a].reshape(240, 320), preferred_element_type=F32)
        snd1[g] = total.astype(BF16).reshape(4, 4, *CHUNK)
        if g == 0:
            pl.semaphore_wait(barrier, 2 * (NX - 1) + 1 + (NY - 1) + (NZ - 1))
        for r in (0, 1, 3, 2):
            q = ((y + (4 - g + 2 * r) % NY) % NY) // 2
            for k in (2, 1, 3):
                send(snd1.at[g, (x + k) % NX, q], rcvx1.at[g, r, k - 1], 0, rx1.at[g, r], at_x(k, core))

    loads[3].wait()
    send(w2.at[core], w2.at[core], 5, swap_sem.at[0], partner)
    loads[4].wait()
    send(wm.at[core], wm.at[core], 6, swap_sem.at[1], partner)

    own = None
    for g in range(2):
        for r in (0, 1, 3, 2):
            k = (4 - g + 2 * r) % NY
            q = ((y + k) % NY) // 2
            wait(rcvx1.at[g, r], rx1.at[g, r])
            total = snd1[g, x, q].astype(F32)
            for other in range(NX - 1):
                total = total + rcvx1[g, r, other].astype(F32)
            if k == 0:
                own = total
            else:
                ybuf1[k - 1] = total.astype(BF16)
                send(ybuf1.at[k - 1], rcvy1.at[k - 1], 1, ry1, at_y(k))
    wait(rcvy1, ry1)
    for k in range(NY - 1):
        own = own + rcvy1[k].astype(F32)
    mine[...] = own.astype(BF16)

    for k in FAR:
        send(mine, agbuf.at[k - 1], 2, ay.at[k - 1], at_y(k))
    sub = x // IMGS
    for k in (0, 1, 7, 2, 6, 3, 5, 4):
        origin = (y - k + NY) % NY
        q = origin // 2
        to_core = 1 - origin % 2
        here = hid.at[core, x, q]
        if k == 0:
            src = mine
        else:
            src = agbuf.at[k - 1]
            wait(src, ay.at[k - 1])
        for kx in (2, 1, 3):
            send(src, here, 3, ax.at[sub], at_x(kx, to_core))

        @pl.when(to_core == core)
        def _():
            pltpu.make_async_copy(src, here, ax.at[sub]).start()

        @pl.when(to_core != core)
        def _():
            send(src, here, 3, ax.at[sub], partner)

    wait(w2.at[0], swap_sem.at[0])
    for t in range(SUBS):
        wait(hid.at[:, t * IMGS : (t + 1) * IMGS], ax.at[t])
        rows = IMGS * 64
        parts = [jnp.zeros((rows, 160), F32) for _ in range(3)]
        place = lax.broadcasted_iota(jnp.int32, (rows // 8, 8, 320), 1)
        for j in range(2):
            block = hid[j, t * IMGS : (t + 1) * IMGS].reshape(rows, 320)
            rect = jnp.maximum(block.astype(F32), 0.0).reshape(rows // 8, 8, 320)
            left = jnp.where(place == 0, 0.0, pltpu.roll(rect, 1, 1))
            right = jnp.where(place == 7, 0.0, pltpu.roll(rect, 7, 1))
            shifted = [v.reshape(rows, 320).astype(BF16) for v in (left, rect, right)]
            for a in range(3):
                for b in range(3):
                    parts[a] = parts[a] + nt(shifted[b], w2[j, a, b])
        parts = [v.reshape(IMGS, 64, 160) for v in parts]
        gap = jnp.zeros((IMGS, 8, 160), F32)
        inner = (
            parts[1]
            + jnp.concatenate([gap, parts[0][:, :56]], 1)
            + jnp.concatenate([parts[2][:, 8:], gap], 1)
        )
        zsnd[t] = inner.astype(BF16).reshape(NZ, ZROWS, 160)
        for k in FAR:
            send(zsnd.at[t, (z + k) % NZ], rcvz.at[t, k - 1], 4, rz.at[t], at_z(k))

    for t in range(SUBS):
        wait(rcvz.at[t], rz.at[t])
        total = zsnd[t, z].astype(F32)
        for k in range(NZ - 1):
            total = total + rcvz[t, k].astype(F32)
        gat[t, z] = jnp.maximum(total, 0.0).astype(BF16)
        for to_z in (0, 1, 2, 3, 7, 6, 5, 4):

            @pl.when(to_z != z)
            def _():
                send(gat.at[t, z], gat.at[t, z], 4, az.at[t], at_z(to_z - z + NZ))

    apart = (core + y) % 2
    wait(wm.at[0], swap_sem.at[1])
    for t in range(SUBS):
        wait(gat.at[t, 0 : NZ - 1], az.at[t])
        gated = gat[t].reshape(IMGS * 64, 160)
        for j in range(2):
            mixed = jnp.dot(gated, wm[j], preferred_element_type=F32).astype(BF16)
            snd3[j, t * IMGS : (t + 1) * IMGS] = mixed.reshape(IMGS, 4, *CHUNK)
        for r in (0, 1, 3, 2):
            k = (4 - apart + 2 * r) % NY
            q = ((y + k) % NY) // 2
            for to_x in range(t * IMGS, (t + 1) * IMGS):

                @pl.when(x != to_x)
                def _():
                    kx = (to_x - x + NX) % NX
                    for j in range(2):
                        send(snd3.at[j, to_x, q], rcvx3.at[k, kx], 0, rx3.at[k], at_x(kx, j))

                @pl.when(x == to_x)
                def _():
                    send(snd3.at[1 - core, to_x, q], rcvx3.at[k, 0], 0, rx3.at[k], partner)
                    pltpu.make_async_copy(snd3.at[core, to_x, q], rcvx3.at[k, 0], rx3.at[k]).start()

    own = None
    for k in (4, 3, 6, 5, 2, 1, 7, 0):
        wait(rcvx3.at[k], rx3.at[k])
        total = rcvx3[k, 0].astype(F32)
        for other in range(1, NX):
            total = total + rcvx3[k, other].astype(F32)
        if k == 0:
            own = total
        else:
            ybuf3[k - 1] = total.astype(BF16)
            send(ybuf3.at[k - 1], rcvy3.at[k - 1], 1, ry3, at_y(k))
    skip = agbuf[6 * (1 - par)]
    own = own + skip.astype(F32)
    wait(rcvy3, ry3)
    for k in range(NY - 1):
        own = own + rcvy3[k].astype(F32)
    out[0] = own.astype(BF16)

    for _ in range(4):
        wait(agbuf, send_sem.at[3])
    for _ in range(2):
        wait(snd1.at[:, 0:3], send_sem.at[0])
        wait(rcvy1, send_sem.at[1])
        wait(rcvz, send_sem.at[4])
    wait(hid.at[0, 0], send_sem.at[0])
    wait(agbuf, send_sem.at[2])
    wait(w2.at[0], send_sem.at[5])
    wait(wm.at[0], send_sem.at[6])


def solution(mesh):
    def step(images, conv_one, conv_two, mix_weight):
        vmem = functools.partial(pltpu.VMEM, dtype=BF16)
        dma = pltpu.SemaphoreType.DMA
        return pl.pallas_call(
            kernel,
            out_shape=jax.ShapeDtypeStruct((1, *CHUNK), BF16),
            in_specs=[pl.BlockSpec(memory_space=pl.ANY)] * 4,
            out_specs=pl.BlockSpec(memory_space=pltpu.VMEM),
            scratch_shapes=[
                vmem((2, 80, 1024)),
                vmem((3, 3, 80, 320)),
                vmem((2, 3, 3, 160, 320)),
                vmem((2, 160, 320)),
                vmem((192, 768)),
                vmem((3, 256, 240)),
                vmem((2, NX, 4, *CHUNK)),
                vmem((2, 4, NX - 1, *CHUNK)),
                vmem((NY - 1, *CHUNK)),
                vmem((NY - 1, *CHUNK)),
                vmem(CHUNK),
                vmem((NY - 1, *CHUNK)),
                vmem((2, NX, 4, *CHUNK)),
                vmem((SUBS, NZ, ZROWS, 160)),
                vmem((SUBS, NZ - 1, ZROWS, 160)),
                vmem((SUBS, NZ, ZROWS, 160)),
                vmem((2, NX, 4, *CHUNK)),
                vmem((NY, NX, *CHUNK)),
                vmem((NY - 1, *CHUNK)),
                vmem((NY - 1, *CHUNK)),
                dma((5,)),
                dma((7,)),
                dma((2,)),
                dma((2, 4)),
                dma,
                dma((NY - 1,)),
                dma((SUBS,)),
                dma((SUBS,)),
                dma((SUBS,)),
                dma((NY,)),
                dma,
            ],
            compiler_params=pltpu.CompilerParams(
                collective_id=0, has_side_effects=True, vmem_limit_bytes=60 * 2**20
            ),
            name="block",
        )(images, conv_one, conv_two, mix_weight)

    in_specs = (
        P(("section", "dp"), None),
        P(None, None, ("section", "dp"), "chan"),
        P(None, None, ("section", "dp"), "chan"),
        P(("section", "dp"), "chan"),
    )
    out_specs = P("dp", "section", "chan")
    return jax.shard_map(step, mesh=mesh, in_specs=in_specs, out_specs=out_specs, check_vma=False)
```
